256 devices in a mesh: tensor: 8 (over x, core), dp: 32 (over y, z).
Axes of the slice: x: 4, y: 4, z: 8, core: 2. Of those that a mesh axis runs over, the one named last changes fastest.
Arguments:
- tokens: bfloat16 [32768, 6144], P(('dp', 'tensor')), may hold values from -24 to 24
- sample_id: int32 [32, 1024], P('dp'), may hold values from 0 to 7, never falling along the last dimension, each value on 1 to 256 neighbouring positions
- timestep: int32 [32, 8], P('dp'), may hold values from 0 to 31
- step_table: float32 [32, 2, 6144], replicated, may hold values from -3 to 3
- weight: bfloat16 [6144, 3072], P(None, 'tensor'), may hold values from -0.078125 to 0.078125
- grad_q: bfloat16 [32768, 3072], P('dp', 'tensor'), may hold values from -6 to 6
Outputs:
- grad_x: bfloat16 [32768, 6144], P(('dp', 'tensor'))
- grad_weight: float32 [6144, 3072], P('dp', 'tensor')
- grad_table: float32 [32, 2, 6144], replicated
The draws below stay inside these ranges and needn't reach their ends.
Inputs may be any that keep to these rules, and one draw needn't show every extreme that they name: `sample_id`: within each replica the ids never fall along its rows, and each of the 8 samples has rows.
All inputs are finite; a program needn't handle non-finite values.
Results may differ from the reference program's by a relative error of at most 0.02.
Values may be sent and summed in bfloat16 or wider, within the bound.
A program may use at most 192 MiB of HBM per device.

```python
import math
import jax
import jax.numpy as jnp
import numpy as np
from jax import lax

D = 6144
TOK_DEV = 128
SAMP = 8
NSTEPS = 32
QW = 3072
ROWS_REP = 1024
TOKENS = 32768
N_TENSOR = 8
N_DP = 32


def set_ends(values, stream_key, least, top_value):
    dims = values.shape
    place = [jax.random.randint(jax.random.fold_in(stream_key, axis), (), 0, dims[axis]) for axis in range(len(dims))]
    values = values.at[tuple(place)].set(least)
    longest = dims.index(max(dims))
    place[longest] = (place[longest] + 1) % dims[longest]
    return values.at[tuple(place)].set(top_value)


def spiked(drawn, own_key, source, target, shards_of, factor):
    owner, partner = [(jnp.arange(drawn.shape[dim]) // (drawn.shape[dim] // shards_of)).reshape([-1 if axis == dim else 1 for axis in range(drawn.ndim)]) for dim in (source, target)]
    chosen = jax.random.permutation(own_key, shards_of)[partner]
    strong = (owner == chosen) | (owner == (partner + shards_of // 2) % shards_of)
    return jnp.where(strong, factor * drawn, drawn)


def block_scale(stream_key, dims, shards, smallest, high):
    factor_of = 1.0
    for position, shards_of in shards:
        draws = jax.random.uniform(jax.random.fold_in(jax.random.fold_in(stream_key, 6), position), (shards_of,), jnp.float32, smallest / len(shards), high / len(shards))
        factor_of = factor_of * jnp.repeat(jnp.exp(draws), dims[position] // shards_of).reshape((-1,) + (1,) * (len(dims) - 1 - position))
    return factor_of


def length_profile(number_of, total, most, lean):
    weights = [(1 << 20) // math.isqrt(grade ** lean) + 1 for grade in range(2, number_of + 1)]
    surplus, given = total - most - (number_of - 1), [1] * (number_of - 1)
    while surplus > 0:
        candidates = [i for i in range(number_of - 1) if given[i] < most]
        whole, budget = sum([weights[i] for i in candidates]), surplus
        for i in candidates:
            more = min(most - given[i], max(1, budget * weights[i] // whole), surplus)
            given[i] = given[i] + more
            surplus = surplus - more
    return np.array([most] + given)


def ragged(stream_key, count, total, reach, lean):
    if count == 2:
        one = jax.random.randint(stream_key, (), max(1, total - reach), min(reach, total - 1) + 1)
        return jnp.stack([one, total - one])
    tallies = jnp.asarray(length_profile(count, total, reach, lean), jnp.int32)
    pairs = (count - 1) // 2
    giver, receiver = tallies[1:1 + 2 * pairs:2], tallies[2:2 + 2 * pairs:2]
    margin = jnp.minimum(giver - 1, reach - receiver)
    moved = jax.random.randint(jax.random.fold_in(stream_key, 1), (pairs,), 0, 1 << 20) % (margin + 1)
    tallies = tallies.at[1:1 + 2 * pairs:2].set(giver - moved).at[2:2 + 2 * pairs:2].set(receiver + moved)
    return tallies[jax.random.permutation(jax.random.fold_in(stream_key, 2), count)]


def bell_draw(stream_key, dims, deviation, limit, cuts=(), held_as=jnp.bfloat16):
    array = jax.random.normal(stream_key, dims, jnp.float32) * deviation
    if len(cuts) > 0:
        array = block_scale(stream_key, dims, cuts, -0.22, 0.18) * array
    return jnp.clip(array, min=-limit, max=limit).astype(held_as)


def gaussian_with(rng, shape, spread, reach, split, heavy, held_as=jnp.bfloat16):
    result = spread * jax.random.normal(rng, shape, jnp.float32)
    if split:
        result = result * block_scale(rng, shape, split, -0.22, 0.18)
    return jnp.clip(spiked(result, jax.random.fold_in(rng, 3), *heavy), -reach, reach).astype(held_as)


def setup_inputs(seed: int = 0) -> dict:
    keys = jax.random.split(jax.random.key(seed), 7)
    tokens = gaussian_with(keys[0], (TOKENS, D), 1.0, 24.0, ((0, 256),), (0, 1, 256, 6.0))
    sample_id = jax.vmap(lambda own: jnp.searchsorted(jnp.cumsum(ragged(own, SAMP, ROWS_REP, 2 * ROWS_REP // SAMP, 1)), jnp.arange(ROWS_REP), side="right"))(jax.random.split(keys[1], N_DP)).reshape((N_DP, ROWS_REP)).astype(jnp.int32)
    timestep = set_ends(jax.random.randint(keys[2], (N_DP, SAMP), 0, NSTEPS), jax.random.fold_in(keys[2], 1), 0, NSTEPS - 1).astype(jnp.int32)
    step_table = bell_draw(keys[3], (NSTEPS, 2, D), 0.5, 3.0, (), jnp.float32)
    weight = bell_draw(keys[4], (D, QW), D ** -0.5, 0.078125, ((1, 8),))
    grad_q = bell_draw(keys[5], (TOKENS, QW), 1.0, 6.0, ((0, 32), (1, 8)))
    return {"tokens": tokens, "sample_id": sample_id, "timestep": timestep, "step_table": step_table, "weight": weight, "grad_q": grad_q}


def normalize(rows_in):
    widened = rows_in.astype(jnp.float32)
    row_mean = lax.optimization_barrier(jnp.mean(widened, axis=-1, keepdims=True))
    centred = widened - row_mean
    variance = lax.optimization_barrier(jnp.mean(centred * centred, axis=-1, keepdims=True))
    inv_std = lax.rsqrt(variance + 1e-06)
    return (centred * inv_std, inv_std)

def row_steps(block_ids, step_of_sample, step_count):
    samples = step_of_sample.shape[0]
    sample_hot = (block_ids[:, None] == jnp.arange(samples, dtype=jnp.int32)[None, :]).astype(jnp.int32)
    step_of_row = lax.optimization_barrier(jnp.sum(sample_hot * step_of_sample[None, :], axis=1))
    return (step_of_row[:, None] == jnp.arange(step_count, dtype=jnp.int32)[None, :]).astype(jnp.float32)

def modulation(hot_rows, step_table):
    feature_count = step_table.shape[2]
    table_flat = step_table.reshape(step_table.shape[0], 2 * feature_count)
    modulation_rows = jnp.dot(hot_rows, table_flat, precision=lax.Precision.HIGHEST)
    return (modulation_rows[:, :feature_count], modulation_rows[:, feature_count:])

def reference(tokens, sample_id, timestep, step_table, weight, grad_q):
    rows_rep = TOK_DEV * N_TENSOR
    token_rows = tokens.reshape(N_DP, rows_rep, D)
    grad_rows = grad_q.reshape(N_DP, rows_rep, QW)
    group_width = QW // N_TENSOR

    def replica(carry, inputs):
        weight_sum, table_sum = carry
        x_rep, ids_rep, steps_rep, g_rep = inputs
        normed, inv_std = normalize(x_rep)
        hot_rows = row_steps(ids_rep, steps_rep, NSTEPS)
        shifts, scales = modulation(hot_rows, step_table)
        modded = (normed * (1.0 + scales) + shifts).astype(jnp.bfloat16)
        weight_sum = weight_sum + jnp.dot(modded.T, g_rep, preferred_element_type=jnp.float32)
        grad_mod = jnp.zeros((rows_rep, D), jnp.float32)
        for group in range(N_TENSOR):
            lower = group * group_width
            term = jnp.dot(g_rep[:, lower:lower + group_width], weight[:, lower:lower + group_width].T, preferred_element_type=jnp.float32)
            grad_mod = grad_mod + lax.optimization_barrier(term.astype(jnp.bfloat16)).astype(jnp.float32)
        grad_normed = grad_mod * (1.0 + scales)
        mean_grad = lax.optimization_barrier(jnp.mean(grad_normed, axis=-1, keepdims=True))
        mean_proj = lax.optimization_barrier(jnp.mean(grad_normed * normed, axis=-1, keepdims=True))
        grad_x_rep = ((grad_normed - mean_grad - normed * mean_proj) * inv_std).astype(jnp.bfloat16)
        shift_sum = jnp.dot(hot_rows.T, grad_mod, precision=lax.Precision.HIGHEST)
        scale_sum = jnp.dot(hot_rows.T, grad_mod * normed, precision=lax.Precision.HIGHEST)
        table_sum = table_sum + jnp.stack([shift_sum, scale_sum], axis=1)
        return ((weight_sum, table_sum), grad_x_rep)
    initial = (jnp.zeros((D, QW), jnp.float32), jnp.zeros((NSTEPS, 2, D), jnp.float32))
    (weight_total, table_total), grad_x_all = lax.scan(replica, initial, (token_rows, sample_id, timestep, grad_rows))
    return (grad_x_all.reshape(TOKENS, D), weight_total, table_total)
```

```python
import jax
import jax.numpy as jnp
from jax import lax
from jax.experimental import pallas as pl
from jax.experimental.pallas import tpu as pltpu
from jax.sharding import PartitionSpec as P

MESH = pl.DeviceIdType.MESH
F32 = jnp.float32
BF16 = jnp.bfloat16

D = 6144
TOK = 128
ROWS = 1024
STEPS = 32
GW = 384
DS = 768
NT = 8
NDP = 32
WZ = 32
WY = 128
WYO = 256
PR = 96
ROUND = (0, 1, 3, 2)


def rem(a, b):
    return lax.rem(a, jnp.int32(b))


def div(a, b):
    return lax.div(a, jnp.int32(b))


def kernel(
    tok_h, sid_ref, ts_ref, tab_h, w_h, gq_h,
    gx_h, gw_h, gt_h,
    tok, nrm32, nrm16, inv, scl, tab, tab_d, hot3, nd, modt, gq, w, part, rs_r, rs_l, fin_s, fin,
    gmacc, gms, gmr, gxv, gwv, tsum, trecv, ttot, tfull,
    loc, ws, wr, ags, agr, ys, yr, ns, nr, qs, qr, rss, rsr, fs, fr, gs, gr, tse, tre, xs, xr_sem,
):
    t = lax.axis_index("tensor")
    p = lax.axis_index("dp")
    x, c = div(t, 2), rem(t, 2)
    y, z = div(p, 8), rem(p, 8)

    def at(tt, pp):
        return {"tensor": tt, "dp": pp}

    def xc(dx, cc):
        return rem(x + dx, 4) * 2 + cc

    def zy(dy, dz):
        return rem(y + dy, 4) * 8 + rem(z + dz, 8)

    sent = []

    def remote(src, dst, s, r, dev, start=True):
        cp = pltpu.make_async_remote_copy(
            src_ref=src, dst_ref=dst, send_sem=s, recv_sem=r, device_id=dev, device_id_type=MESH
        )
        if start:
            cp.start()
            sent.append(cp)
        return cp

    def arrived(dst, s, r):
        pltpu.make_async_remote_copy(
            src_ref=dst, dst_ref=dst, send_sem=s, recv_sem=r, device_id=at(t, p), device_id_type=MESH
        ).wait_recv()

    bar = pltpu.get_barrier_semaphore()
    for i in range(1, NT):
        pl.semaphore_signal(bar, inc=1, device_id=at(rem(t + i, NT), p), device_id_type=MESH)

    def greet(i, _):
        pl.semaphore_signal(bar, inc=1, device_id=at(t, rem(p + i, NDP)), device_id_type=MESH)
        return 0

    lax.fori_loop(1, NDP, greet, 0)
    for yy in range(4):
        for h in range(2):
            pl.semaphore_signal(
                bar, inc=1, device_id=at(div(p, 4), yy * 8 + 2 * rem(p, 4) + h), device_id_type=MESH
            )

    def cols(cc):
        return pl.ds(pl.multiple_of(cc * GW, GW), GW)

    def slice_cols(tt):
        return pl.ds(pl.multiple_of(tt * DS, DS), DS)

    cp_tok = pltpu.make_async_copy(tok_h, tok, loc.at[0])
    cp_tok.start()
    cp_tab = pltpu.make_async_copy(tab_h, tab, loc.at[1])
    cp_tab.start()
    cp_td = pltpu.make_async_copy(tab_h.at[:, :, slice_cols(t)], tab_d, loc.at[2])
    cp_td.start()
    cp_gq = pltpu.make_async_copy(gq_h, gq.at[x, :, cols(c)], loc.at[3])
    cp_gq.start()
    cp_wz = pltpu.make_async_copy(
        w_h.at[pl.ds(t * DS + z * WZ, WZ), :], w.at[x, pl.ds(z * WZ, WZ), cols(c)], loc.at[4]
    )
    cp_wz.start()
    cp_wy = pltpu.make_async_copy(
        w_h.at[pl.ds(t * DS + WYO + y * WY, WY), :], w.at[x, pl.ds(WYO + y * WY, WY), cols(c)], loc.at[5]
    )
    cp_wy.start()

    pl.semaphore_wait(bar, NT - 1 + NDP - 1 + 8)

    for i in range(1, NT):
        tt = rem(t + i, NT)
        remote(
            w_h.at[pl.ds(tt * DS + z * WZ, WZ), :], w.at[x, pl.ds(z * WZ, WZ), cols(c)],
            ws.at[0, i], wr.at[0, i], at(tt, p),
        )
        remote(
            w_h.at[pl.ds(tt * DS + WYO + y * WY, WY), :], w.at[x, pl.ds(WYO + y * WY, WY), cols(c)],
            ws.at[1, i], wr.at[1, i], at(tt, p),
        )

    cp_tok.wait()

    def norm(i, _):
        rows = pl.ds(i * 16, 16)
        v = tok[rows, :].astype(F32)
        v = v - jnp.mean(v, axis=-1, keepdims=True)
        k = lax.rsqrt(jnp.mean(v * v, axis=-1, keepdims=True) + 1e-06)
        v = v * k
        nrm32[rows, :] = v
        inv[rows, :] = jnp.broadcast_to(k, (16, 128))
        for j in range(NT):
            nrm16[j, rows, :] = v[:, j * DS : (j + 1) * DS].astype(BF16)
        return 0

    lax.fori_loop(0, TOK // 16, norm, 0)
    for i in (4, 5, 2, 3, 6, 7, 1):
        tt = rem(t + i, NT)
        remote(nrm16.at[tt], nd.at[t], ns.at[i], nr.at[i], at(tt, p))
    nd[t] = nrm16[t]

    def half(h):
        return pl.ds(h * 512, 512)

    right, left, sib = at(xc(1, c), p), at(xc(3, c), p), at(xc(0, 1 - c), p)
    remote(gq_h.at[half(0), :], gq.at[x, half(0), cols(c)], qs.at[0], qr.at[0], right)
    remote(gq_h.at[half(1), :], gq.at[x, half(1), cols(c)], qs.at[1], qr.at[1], left)
    remote(gq_h.at[half(1), :], gq.at[x, half(1), cols(c)], qs.at[2], qr.at[2], right)
    remote(gq_h.at[half(0), :], gq.at[x, half(0), cols(c)], qs.at[3], qr.at[3], left)
    remote(gq_h, gq.at[x, :, cols(c)], qs.at[4], qr.at[4], sib)

    step = jnp.zeros((1, ROWS), jnp.int32)
    for s in range(8):
        step = step + jnp.where(sid_ref[...] == s, ts_ref[0:1, s : s + 1], 0)
    hot = (lax.broadcasted_iota(jnp.int32, (STEPS, ROWS), 0) == step).astype(F32).astype(BF16)
    for k in range(3):
        hot3[k * STEPS : (k + 1) * STEPS, :] = hot

    def thirds(v):
        hi = v.astype(BF16)
        rest = v - hi.astype(F32)
        mid = rest.astype(BF16)
        lo = (rest - mid.astype(F32)).astype(BF16)
        return jnp.concatenate([hi, mid, lo], axis=0)

    def pick(h, table):
        return lax.dot_general(h, thirds(table), (((0,), (0,)), ((), ())), preferred_element_type=F32)

    cp_tab.wait()
    own = hot3[:, pl.ds(pl.multiple_of(t * TOK, TOK), TOK)]
    for j in range(NT):
        js = slice(j * DS, (j + 1) * DS)
        scl[:, js] = pick(own, 1.0 + tab[:, 1, js])

    cp_wz.wait()
    for i in range(1, NT):
        s = rem(t + NT - i, NT)
        arrived(w.at[div(s, 2), pl.ds(z * WZ, WZ), cols(rem(s, 2))], ws.at[0, i], wr.at[0, i])

    def wz(d, k=None):
        r = pl.ds(rem(z + d + 8, 8) * WZ, WZ)
        return w.at[:, r, :] if k is None else w.at[pl.ds(2 * k, 2), r, :]

    def gather_z(s):
        a, b = (wz(-s), wz(s)) if s < 3 else (wz(-s, 0), wz(s, 1))
        remote(a, a, ags.at[0, s], agr.at[0, s], at(t, zy(0, 1)))
        remote(b, b, ags.at[1, s], agr.at[1, s], at(t, zy(0, 7)))

    def gathered_z(s):
        a, b = (wz(-1 - s), wz(1 + s)) if s < 3 else (wz(-1 - s, 0), wz(1 + s, 1))
        arrived(a, ags.at[0, s], agr.at[0, s])
        arrived(b, ags.at[1, s], agr.at[1, s])

    def wy(d):
        return w.at[:, pl.ds(WYO + rem(y + d, 4) * WY, WY), :]

    gather_z(0)
    cp_wy.wait()
    for i in range(1, NT):
        s = rem(t + NT - i, NT)
        arrived(w.at[div(s, 2), pl.ds(WYO + y * WY, WY), cols(rem(s, 2))], ws.at[1, i], wr.at[1, i])
    for i in (1, 3, 2):
        remote(wy(0), wy(0), ys.at[i], yr.at[i], at(t, zy(i, 0)))
    for s in range(3):
        gathered_z(s)
        gather_z(s + 1)

    for i in range(1, NT):
        arrived(nd.at[rem(t + NT - i, NT)], ns.at[i], nr.at[i])
    cp_td.wait()
    shift3 = thirds(tab_d[:, 0, :])
    scale3 = thirds(1.0 + tab_d[:, 1, :])

    for i in range(4):
        h = hot3[:, i * 256 : (i + 1) * 256]
        sh = lax.dot_general(h, shift3, (((0,), (0,)), ((), ())), preferred_element_type=F32)
        sc = lax.dot_general(h, scale3, (((0,), (0,)), ((), ())), preferred_element_type=F32)
        m = nd[2 * i : 2 * i + 2].reshape(256, DS).astype(F32) * sc + sh
        modt[:, i * 256 : (i + 1) * 256] = m.T.astype(BF16)

    def partial(r):
        xx = rem(x + ROUND[r], 4)

        def rowblock(i, _):
            rows = pl.ds(pl.multiple_of(i * 256, 256), 256)
            part[r, rows, :] = jnp.dot(modt[rows, :], gq[xx], preferred_element_type=F32).astype(BF16)
            return 0

        lax.fori_loop(0, 3, rowblock, 0)

    A, B = slice(0, GW), slice(GW, DS)

    def piece(d):
        return pl.ds(pl.multiple_of(rem(z + d + 8, 8) * PR, PR), PR)

    def rs_send(r, s):
        if s == 0:
            a = (part.at[r, piece(4), A], rs_r.at[r, s, :, A])
            b = (part.at[r, piece(4), B], rs_l.at[r, s, :, B])
        else:
            a = (part.at[r, piece(4 - s), :], rs_r.at[r, s])
            b = (part.at[r, piece(s - 4), :], rs_l.at[r, s])
        remote(*a, rss.at[0, r, s], rsr.at[0, r, s], at(t, zy(0, 1)))
        remote(*b, rss.at[1, r, s], rsr.at[1, r, s], at(t, zy(0, 7)))

    def add(r, pc, cc, got):
        part[r, pc, cc] = (part[r, pc, cc].astype(F32) + got.astype(F32)).astype(BF16)

    def rs_step(r, s):
        if s == 0:
            arrived(rs_r.at[r, s, :, A], rss.at[0, r, s], rsr.at[0, r, s])
            add(r, piece(3), A, rs_r[r, s, :, A])
            arrived(rs_l.at[r, s, :, B], rss.at[1, r, s], rsr.at[1, r, s])
            add(r, piece(-3), B, rs_l[r, s, :, B])
        elif s < 3:
            arrived(rs_r.at[r, s], rss.at[0, r, s], rsr.at[0, r, s])
            add(r, piece(3 - s), slice(None), rs_r[r, s])
            arrived(rs_l.at[r, s], rss.at[1, r, s], rsr.at[1, r, s])
            add(r, piece(s - 3), slice(None), rs_l[r, s])
        if s < 3:
            rs_send(r, s + 1)
            return
        arrived(rs_r.at[r, s], rss.at[0, r, s], rsr.at[0, r, s])
        arrived(rs_l.at[r, s], rss.at[1, r, s], rsr.at[1, r, s])
        v = part[r, piece(0), :].astype(F32) + rs_r[r, s].astype(F32) + rs_l[r, s].astype(F32)
        xx = rem(x + ROUND[r], 4)
        pp = 4 * t + div(z, 2)
        for k in range(2):
            fin_s[r, k] = v[:, k * GW : (k + 1) * GW].astype(BF16)
            dst, rs = fin.at[y, rem(z, 2)], fr.at[y, rem(z, 2)]
            if r > 0:
                remote(fin_s.at[r, k], dst, fs.at[r, k], rs, at(2 * xx + k, pp))
            else:
                me = jnp.logical_and(pp == p, c == k)

                @pl.when(me)
                def _():
                    pltpu.make_async_copy(fin_s.at[r, k], dst, rs).start()

                @pl.when(jnp.logical_not(me))
                def _():
                    remote(fin_s.at[r, k], dst, fs.at[r, k], rs, at(2 * xx + k, pp))
                    sent.pop()

    def gm_add(xx, first):
        def rowblock(i, _):
            rows = pl.ds(pl.multiple_of(i * 256, 256), 256)
            v = lax.dot_general(gq[xx, rows, :], w[xx], (((1,), (1,)), ((), ())), preferred_element_type=F32)
            gmacc[rows, :] = v if first else gmacc[rows, :] + v
            return 0

        lax.fori_loop(0, 4, rowblock, 0)

    def forward(xx, hh, k):
        v = gq.at[xx, hh, cols(c)]
        remote(v, v, qs.at[k], qr.at[k], sib)

    def got(xx, hh, cc, k):
        arrived(gq.at[xx, hh, cols(cc)], qs.at[k], qr.at[k])

    x1, x2, x3 = rem(x + 1, 4), rem(x + 2, 4), rem(x + 3, 4)
    full = pl.ds(0, ROWS)
    cp_gq.wait()
    got(x, full, 1 - c, 4)
    partial(0)
    rs_send(0, 0)
    gathered_z(3)
    for i in (1, 3, 2):
        arrived(wy(4 - i), ys.at[i], yr.at[i])
    rs_step(0, 0)
    gm_add(x, True)
    rs_step(0, 1)
    rs_step(0, 2)
    got(x3, half(0), c, 0)
    remote(gq.at[x3, half(0), cols(c)], gq.at[x3, half(0), cols(c)], qs.at[5], qr.at[5], right)
    forward(x3, half(0), 7)
    got(x1, half(1), c, 1)
    remote(gq.at[x1, half(1), cols(c)], gq.at[x1, half(1), cols(c)], qs.at[6], qr.at[6], left)
    forward(x1, half(1), 8)
    rs_step(0, 3)
    got(x3, half(1), c, 2)
    forward(x3, half(1), 9)
    got(x1, half(0), c, 3)
    forward(x1, half(0), 10)
    got(x1, half(1), 1 - c, 8)
    got(x1, half(0), 1 - c, 10)
    partial(1)
    rs_send(1, 0)
    got(x3, half(0), 1 - c, 7)
    got(x3, half(1), 1 - c, 9)
    partial(2)
    rs_send(2, 0)
    rs_step(1, 0)
    rs_step(2, 0)
    gm_add(x1, False)
    rs_step(1, 1)
    gm_add(x3, False)
    rs_step(2, 1)
    got(x2, half(0), c, 5)
    forward(x2, half(0), 11)
    got(x2, half(1), c, 6)
    forward(x2, half(1), 12)
    rs_step(1, 2)
    got(x2, half(0), 1 - c, 11)
    got(x2, half(1), 1 - c, 12)

    for k in (2, 1, 3, 0):
        xx = rem(x + k, 4)
        rows = pl.ds(pl.multiple_of(xx * 256, 256), 256)
        v = lax.dot_general(gq[x2, rows, :], w[x2], (((1,), (1,)), ((), ())), preferred_element_type=F32)
        v = gmacc[rows, :] + v
        gms[pl.ds(2 * xx, 2)] = v.astype(BF16).reshape(2, TOK, DS)
        for cc in range(2):
            tt = 2 * xx + (c if cc == 0 else 1 - c)
            if k == 0 and cc == 0:
                gmr[t] = gms[t]
            else:
                remote(gms.at[tt], gmr.at[t], gs.at[k, cc], gr.at[k, cc], at(tt, p))
    partial(3)
    rs_send(3, 0)
    rs_step(2, 2)
    rs_step(1, 3)

    hot1 = hot3[0:STEPS, :]
    gmv = gms[...].reshape(ROWS, DS)
    tsum[:, 0, :] = jnp.dot(hot1, gmv, preferred_element_type=F32)
    prod = (gmv.astype(F32) * nd[...].reshape(ROWS, DS).astype(F32)).astype(BF16)
    tsum[:, 1, :] = jnp.dot(hot1, prod, preferred_element_type=F32)
    cp_t0 = pltpu.make_async_copy(tsum.at[p], trecv.at[p], tre.at[0])
    cp_t0.start()

    def scatter(i, _):
        q = rem(p + i, NDP)
        pltpu.make_async_remote_copy(
            src_ref=tsum.at[q], dst_ref=trecv.at[p], send_sem=tse.at[0], recv_sem=tre.at[0],
            device_id=at(t, q), device_id_type=MESH,
        ).start()
        return 0

    lax.fori_loop(1, NDP, scatter, 0)
    rs_step(3, 0)
    rs_step(2, 3)
    rs_step(3, 1)
    pltpu.make_async_copy(trecv, trecv, tre.at[0]).wait()
    ttot[...] = jnp.sum(trecv[...], axis=0)
    cp_t1 = pltpu.make_async_copy(ttot, tfull.at[p], tre.at[1])
    cp_t1.start()

    def spread(i, _):
        q = rem(p + i, NDP)
        pltpu.make_async_remote_copy(
            src_ref=ttot, dst_ref=tfull.at[p], send_sem=tse.at[1], recv_sem=tre.at[1],
            device_id=at(t, q), device_id_type=MESH,
        ).start()
        return 0

    lax.fori_loop(1, NDP, spread, 0)
    rs_step(3, 2)
    rs_step(3, 3)
    pltpu.make_async_copy(tfull, tfull, tre.at[1]).wait()

    def gt(tt):
        return gt_h.at[:, :, slice_cols(tt)]

    cp_gt = pltpu.make_async_copy(tfull, gt(t), loc.at[6])
    cp_gt.start()
    for k in (2, 1, 3):
        remote(tfull, gt(t), xs.at[k], xr_sem.at[k], at(xc(k, c), p))
    remote(tfull, gt(t), xs.at[0], xr_sem.at[0], sib)

    for k in (1, 3, 2, 0):
        for cc in range(2):
            if k == 0 and cc == 0:
                continue
            arrived(gmr.at[2 * rem(x + 4 - k, 4) + (c if cc == 0 else 1 - c)], gs.at[k, cc], gr.at[k, cc])

    def back(i, _):
        rows = pl.ds(i * 16, 16)
        gn = [gmr[j, rows, :].astype(F32) * scl[rows, j * DS : (j + 1) * DS] for j in range(NT)]
        nv = [nrm32[rows, j * DS : (j + 1) * DS] for j in range(NT)]
        m1 = sum(jnp.sum(g, axis=-1, keepdims=True) for g in gn) * (1.0 / D)
        m2 = sum(jnp.sum(g * n, axis=-1, keepdims=True) for g, n in zip(gn, nv)) * (1.0 / D)
        k = inv[rows, 0:1]
        for j in range(NT):
            gxv[rows, j * DS : (j + 1) * DS] = ((gn[j] - m1 - nv[j] * m2) * k).astype(BF16)
        return 0

    lax.fori_loop(0, TOK // 16, back, 0)
    cp_gx = pltpu.make_async_copy(gxv, gx_h, loc.at[7])
    cp_gx.start()

    for k in (1, 3, 2):
        s = xc(4 - k, c)
        arrived(gt(s), xs.at[k], xr_sem.at[k])
        remote(gt(s), gt(s), xs.at[3 + k], xr_sem.at[3 + k], sib)

    for h in range(2):
        for yy in range(4):
            arrived(fin.at[yy, h], fs.at[0, 0], fr.at[yy, h])
        gwv[h * PR : (h + 1) * PR, :] = sum(fin[yy, h].astype(F32) for yy in range(4))
    cp_gw = pltpu.make_async_copy(gwv, gw_h, loc.at[8])
    cp_gw.start()

    arrived(gt(xc(0, 1 - c)), xs.at[0], xr_sem.at[0])
    for k in (1, 3, 2):
        s = xc(4 - k, 1 - c)
        arrived(gt(s), xs.at[3 + k], xr_sem.at[3 + k])
    cp_gt.wait()
    cp_gx.wait()
    cp_gw.wait()
    for cp in sent:
        cp.wait_send()
    for k in range(2):
        me = jnp.logical_and(4 * t + div(z, 2) == p, c == k)

        @pl.when(jnp.logical_not(me))
        def _():
            remote(fin_s.at[0, k], fin.at[y, rem(z, 2)], fs.at[0, k], fr.at[y, rem(z, 2)], at(2 * x + k, p), start=False).wait_send()

    pltpu.make_async_copy(trecv.at[pl.ds(0, NDP - 1)], trecv.at[pl.ds(0, NDP - 1)], tse.at[0]).wait()
    pltpu.make_async_copy(trecv.at[pl.ds(0, NDP - 1)], trecv.at[pl.ds(0, NDP - 1)], tse.at[1]).wait()


def body(tokens, sample_id, timestep, step_table, weight, grad_q):
    any_spec = pl.BlockSpec(memory_space=pl.ANY)
    vmem_spec = pl.BlockSpec(memory_space=pltpu.VMEM)
    dma = pltpu.SemaphoreType.DMA
    return pl.pallas_call(
        kernel,
        name="fused_backward",
        out_shape=(
            jax.ShapeDtypeStruct((TOK, D), BF16),
            jax.ShapeDtypeStruct((2 * PR, GW), F32),
            jax.ShapeDtypeStruct((STEPS, 2, D), F32),
        ),
        in_specs=[any_spec, vmem_spec, vmem_spec, any_spec, any_spec, any_spec],
        out_specs=(any_spec, any_spec, any_spec),
        scratch_shapes=[
            pltpu.VMEM((TOK, D), BF16),
            pltpu.VMEM((TOK, D), F32),
            pltpu.VMEM((NT, TOK, DS), BF16),
            pltpu.VMEM((TOK, 128), F32),
            pltpu.VMEM((TOK, D), F32),
            pltpu.VMEM((STEPS, 2, D), F32),
            pltpu.VMEM((STEPS, 2, DS), F32),
            pltpu.VMEM((3 * STEPS, ROWS), BF16),
            pltpu.VMEM((NT, TOK, DS), BF16),
            pltpu.VMEM((DS, ROWS), BF16),
            pltpu.VMEM((4, ROWS, DS), BF16),
            pltpu.VMEM((4, DS, DS), BF16),
            pltpu.VMEM((4, DS, DS), BF16),
            pltpu.VMEM((4, 4, PR, DS), BF16),
            pltpu.VMEM((4, 4, PR, DS), BF16),
            pltpu.VMEM((4, 2, PR, GW), BF16),
            pltpu.VMEM((4, 2, PR, GW), BF16),
            pltpu.VMEM((ROWS, DS), F32),
            pltpu.VMEM((NT, TOK, DS), BF16),
            pltpu.VMEM((NT, TOK, DS), BF16),
            pltpu.VMEM((TOK, D), BF16),
            pltpu.VMEM((2 * PR, GW), F32),
            pltpu.VMEM((STEPS, 2, DS), F32),
            pltpu.VMEM((NDP, 2, DS), F32),
            pltpu.VMEM((2, DS), F32),
            pltpu.VMEM((STEPS, 2, DS), F32),
            dma((9,)),
            dma((2, NT)), dma((2, NT)),
            dma((2, 4)), dma((2, 4)),
            dma((4,)), dma((4,)),
            dma((NT,)), dma((NT,)),
            dma((13,)), dma((13,)),
            dma((2, 4, 4)), dma((2, 4, 4)),
            dma((4, 2)), dma((4, 2)),
            dma((4, 2)), dma((4, 2)),
            dma((2,)), dma((2,)),
            dma((7,)), dma((7,)),
        ],
        cost_estimate=pl.CostEstimate(flops=9_700_000_000, bytes_accessed=14_000_000, transcendentals=0),
        compiler_params=pltpu.CompilerParams(
            collective_id=0, has_side_effects=True, vmem_limit_bytes=60 * 2**20
        ),
    )(tokens, sample_id, timestep, step_table, weight, grad_q)


def solution(mesh):
    placed = (
        P(("dp", "tensor"), None),
        P("dp", None),
        P("dp", None),
        P(),
        P(None, "tensor"),
        P("dp", "tensor"),
    )
    return jax.shard_map(
        body,
        mesh=mesh,
        in_specs=placed,
        out_specs=(P(("dp", "tensor"), None), P("dp", "tensor"), P()),
        check_vma=False,
    )
```

```python
import jax
import jax.numpy as jnp
from jax import lax
from jax.experimental import pallas as pl
from jax.experimental.pallas import tpu as pltpu
from jax.sharding import PartitionSpec as P

MESH = pl.DeviceIdType.MESH
F32 = jnp.float32
BF16 = jnp.bfloat16

D = 6144
TOK = 128
ROWS = 1024
STEPS = 32
GW = 384
DS = 768
NT = 8
NDP = 32
WZ = 64
WY = 64
WYO = 512
PY = 192
PZ = 48
ROUND = (0, 1, 3, 2)


def rem(a, b):
    return lax.rem(a, jnp.int32(b))


def div(a, b):
    return lax.div(a, jnp.int32(b))


def kernel(
    tok_h, sid_ref, ts_ref, tab_h, w_h, gq_h,
    gx_h, gw_h, gt_h,
    tok, nrm32, nrm16, inv, scl, tab, tab_d, hot3, nd, modt, gq, w, part, y0, y1, zs, zr, fin, gwr, gwv,
    gmacc, gms, gmr, gxv, tsum, tz, tp, ty, tt_v, tfull, tb,
    loc, ws, wr, ags, agr, ys, yr, ns, nr, qs, qr, rss, rsr, zss, zsr, fs, fr, gs, gr, tse, tre, tys, tyr, xs, xr_sem,
):
    t = lax.axis_index("tensor")
    p = lax.axis_index("dp")
    x, c = div(t, 2), rem(t, 2)
    y, z = div(p, 8), rem(p, 8)

    def at(tt, pp):
        return {"tensor": tt, "dp": pp}

    def xc(dx, cc):
        return rem(x + dx, 4) * 2 + cc

    def zy(dy, dz):
        return rem(y + dy, 4) * 8 + rem(z + dz, 8)

    sent = []

    def remote(src, dst, s, r, dev, start=True):
        cp = pltpu.make_async_remote_copy(
            src_ref=src, dst_ref=dst, send_sem=s, recv_sem=r, device_id=dev, device_id_type=MESH
        )
        if start:
            cp.start()
            sent.append(cp)
        return cp

    def arrived(dst, s, r):
        pltpu.make_async_remote_copy(
            src_ref=dst, dst_ref=dst, send_sem=s, recv_sem=r, device_id=at(t, p), device_id_type=MESH
        ).wait_recv()

    bar = pltpu.get_barrier_semaphore()
    for i in range(1, NT):
        pl.semaphore_signal(bar, inc=1, device_id=at(rem(t + i, NT), p), device_id_type=MESH)

    for i in range(1, 8):
        pl.semaphore_signal(bar, inc=1, device_id=at(t, zy(0, i)), device_id_type=MESH)
    for i in range(1, 4):
        pl.semaphore_signal(bar, inc=1, device_id=at(t, zy(i, 0)), device_id_type=MESH)
    for q in range(4):
        pl.semaphore_signal(
            bar, inc=1, device_id=at(div(p, 4), rem(p, 4) * 8 + 2 * q + c), device_id_type=MESH
        )

    def cols(cc):
        return pl.ds(pl.multiple_of(cc * GW, GW), GW)

    def slice_cols(tt):
        return pl.ds(pl.multiple_of(tt * DS, DS), DS)

    cp_tok = pltpu.make_async_copy(tok_h, tok, loc.at[0])
    cp_tok.start()
    cp_tab = pltpu.make_async_copy(tab_h, tab, loc.at[1])
    cp_tab.start()
    cp_td = pltpu.make_async_copy(tab_h.at[:, :, slice_cols(t)], tab_d, loc.at[2])
    cp_td.start()
    cp_gq = pltpu.make_async_copy(gq_h, gq.at[x, :, cols(c)], loc.at[3])
    cp_gq.start()
    cp_wz = pltpu.make_async_copy(
        w_h.at[pl.ds(t * DS + z * WZ, WZ), :], w.at[x, pl.ds(z * WZ, WZ), cols(c)], loc.at[4]
    )
    cp_wz.start()
    cp_wy = pltpu.make_async_copy(
        w_h.at[pl.ds(t * DS + WYO + y * WY, WY), :], w.at[x, pl.ds(WYO + y * WY, WY), cols(c)], loc.at[5]
    )
    cp_wy.start()

    pl.semaphore_wait(bar, NT - 1 + 7 + 3 + 4)

    for i in range(1, NT):
        tt = rem(t + i, NT)
        remote(
            w_h.at[pl.ds(tt * DS + z * WZ, WZ), :], w.at[x, pl.ds(z * WZ, WZ), cols(c)],
            ws.at[0, i], wr.at[0, i], at(tt, p),
        )
        remote(
            w_h.at[pl.ds(tt * DS + WYO + y * WY, WY), :], w.at[x, pl.ds(WYO + y * WY, WY), cols(c)],
            ws.at[1, i], wr.at[1, i], at(tt, p),
        )

    cp_tok.wait()

    def norm(i, _):
        rows = pl.ds(i * 16, 16)
        v = tok[rows, :].astype(F32)
        v = v - jnp.mean(v, axis=-1, keepdims=True)
        k = lax.rsqrt(jnp.mean(v * v, axis=-1, keepdims=True) + 1e-06)
        v = v * k
        nrm32[rows, :] = v
        inv[rows, :] = jnp.broadcast_to(k, (16, 128))
        for j in range(NT):
            nrm16[j, rows, :] = v[:, j * DS : (j + 1) * DS].astype(BF16)
        return 0

    lax.fori_loop(0, TOK // 16, norm, 0)
    for i in (4, 5, 2, 3, 6, 7, 1):
        tt = rem(t + i, NT)
        remote(nrm16.at[tt], nd.at[t], ns.at[i], nr.at[i], at(tt, p))
    nd[t] = nrm16[t]

    def half(h):
        return pl.ds(h * 512, 512)

    right, left, sib = at(xc(1, c), p), at(xc(3, c), p), at(xc(0, 1 - c), p)

    step = jnp.zeros((1, ROWS), jnp.int32)
    for s in range(8):
        step = step + jnp.where(sid_ref[...] == s, ts_ref[0:1, s : s + 1], 0)
    level = lax.broadcasted_iota(jnp.int32, (2 * STEPS, ROWS), 0)
    hot_shift = (level == 2 * step).astype(F32).astype(BF16)
    hot_scale = (level == 2 * step + 1).astype(F32).astype(BF16)
    hot = (lax.broadcasted_iota(jnp.int32, (STEPS, ROWS), 0) == step).astype(F32).astype(BF16)
    for k in range(3):
        hot3[k * STEPS : (k + 1) * STEPS, :] = hot

    def thirds(v):
        hi = v.astype(BF16)
        rest = v - hi.astype(F32)
        mid = rest.astype(BF16)
        lo = (rest - mid.astype(F32)).astype(BF16)
        return jnp.concatenate([hi, mid, lo], axis=0)

    def pick(h, table):
        return lax.dot_general(h, thirds(table), (((0,), (0,)), ((), ())), preferred_element_type=F32)

    cp_tab.wait()
    own = hot3[:, pl.ds(pl.multiple_of(t * TOK, TOK), TOK)]
    for j in range(NT):
        js = slice(j * DS, (j + 1) * DS)
        scl[:, js] = pick(own, 1.0 + tab[:, 1, js])

    def forward(xx, hh, k):
        v = gq.at[xx, hh, cols(c)]
        remote(v, v, qs.at[k], qr.at[k], sib)

    def got(xx, hh, cc, k):
        arrived(gq.at[xx, hh, cols(cc)], qs.at[k], qr.at[k])

    x1, x2, x3 = rem(x + 1, 4), rem(x + 2, 4), rem(x + 3, 4)

    def arrived_rows(which):
        for i in which:
            arrived(nd.at[rem(t + NT - i, NT)], ns.at[i], nr.at[i])

    cp_wz.wait()
    for i in range(1, NT):
        s = rem(t + NT - i, NT)
        arrived(w.at[div(s, 2), pl.ds(z * WZ, WZ), cols(rem(s, 2))], ws.at[0, i], wr.at[0, i])

    def wz(d, k=None):
        r = pl.ds(rem(z + d + 8, 8) * WZ, WZ)
        return w.at[:, r, :] if k is None else w.at[pl.ds(2 * k, 2), r, :]

    def gather_z(s):
        a, b = (wz(-s), wz(s)) if s < 3 else (wz(-s, 0), wz(s, 1))
        remote(a, a, ags.at[0, s], agr.at[0, s], at(t, zy(0, 1)))
        remote(b, b, ags.at[1, s], agr.at[1, s], at(t, zy(0, 7)))

    def gathered_z(s):
        a, b = (wz(-1 - s), wz(1 + s)) if s < 3 else (wz(-1 - s, 0), wz(1 + s, 1))
        arrived(a, ags.at[0, s], agr.at[0, s])
        arrived(b, ags.at[1, s], agr.at[1, s])

    def wy(d):
        return w.at[:, pl.ds(WYO + rem(y + d, 4) * WY, WY), :]

    gather_z(0)
    cp_wy.wait()
    for i in range(1, NT):
        s = rem(t + NT - i, NT)
        arrived(w.at[div(s, 2), pl.ds(WYO + y * WY, WY), cols(rem(s, 2))], ws.at[1, i], wr.at[1, i])
    for i in (1, 3, 2):
        remote(wy(0), wy(0), ys.at[i], yr.at[i], at(t, zy(i, 0)))
    arrived_rows((2, 6))
    remote(gq_h.at[half(0), :], gq.at[x, half(0), cols(c)], qs.at[0], qr.at[0], right)
    remote(gq_h.at[half(1), :], gq.at[x, half(1), cols(c)], qs.at[1], qr.at[1], left)
    remote(gq_h.at[half(1), :], gq.at[x, half(1), cols(c)], qs.at[2], qr.at[2], right)
    remote(gq_h.at[half(0), :], gq.at[x, half(0), cols(c)], qs.at[3], qr.at[3], left)
    remote(gq_h, gq.at[x, :, cols(c)], qs.at[4], qr.at[4], sib)
    gathered_z(0)
    gather_z(1)

    arrived_rows((1, 3, 4, 5, 7))
    cp_td.wait()
    shift3 = thirds(tab_d[:, 0, :])
    scale3 = thirds(1.0 + tab_d[:, 1, :])

    for i in range(4):
        h = hot3[:, i * 256 : (i + 1) * 256]
        sh = lax.dot_general(h, shift3, (((0,), (0,)), ((), ())), preferred_element_type=F32)
        sc = lax.dot_general(h, scale3, (((0,), (0,)), ((), ())), preferred_element_type=F32)
        m = nd[2 * i : 2 * i + 2].reshape(256, DS).astype(F32) * sc + sh
        modt[:, i * 256 : (i + 1) * 256] = m.T.astype(BF16)

    def partial(r):
        xx = rem(x + ROUND[r], 4)

        def rowblock(i, _):
            rows = pl.ds(pl.multiple_of(i * 256, 256), 256)
            part[r, rows, :] = jnp.dot(modt[rows, :], gq[xx], preferred_element_type=F32).astype(BF16)
            return 0

        lax.fori_loop(0, 3, rowblock, 0)

    A, B = slice(0, GW), slice(GW, DS)
    up, down = at(t, zy(1, 0)), at(t, zy(3, 0))

    def piece(d):
        return pl.ds(pl.multiple_of(rem(y + d, 4) * PY, PY), PY)

    def y_send(r):
        for k, (d, cc, dst, dev) in enumerate(
            ((2, A, y0.at[0, r], up), (1, B, y1.at[0, r, :, B], up))
        ):
            remote(part.at[r, piece(d), cc], dst, rss.at[0, r, k], rsr.at[0, r, k], dev)
        for k, (d, cc, dst, dev) in enumerate(
            ((2, B, y0.at[1, r], down), (3, A, y1.at[1, r, :, A], down))
        ):
            remote(part.at[r, piece(d), cc], dst, rss.at[1, r, k], rsr.at[1, r, k], dev)

    def y_pass(r):
        for k, (d, cc, dev) in enumerate(((1, A, up), (3, B, down))):
            arrived(y0.at[k, r], rss.at[k, r, 0], rsr.at[k, r, 0])
            v = part[r, piece(d), cc].astype(F32) + y0[k, r].astype(F32)
            part[r, piece(d), cc] = v.astype(BF16)
            remote(part.at[r, piece(d), cc], y1.at[k, r, :, cc], rss.at[k, r, 2], rsr.at[k, r, 2], dev)

    def z_send(r):
        for k, (early, late) in enumerate(((B, A), (A, B))):
            arrived(y1.at[k, r, :, early], rss.at[k, r, 1], rsr.at[k, r, 1])
            arrived(y1.at[k, r, :, late], rss.at[k, r, 2], rsr.at[k, r, 2])
        v = part[r, piece(0), :].astype(F32) + y1[0, r].astype(F32) + y1[1, r].astype(F32)
        for k in range(8):
            rows, cc = slice((k // 2) * PZ, (k // 2 + 1) * PZ), (A, B)[k % 2]
            zs[r, k] = v[rows, cc].astype(BF16)
        pltpu.make_async_copy(zs.at[r, z], zr.at[r, z], zsr.at[r]).start()

        def spread_z(i, _):
            zz = rem(z + i, 8)
            pltpu.make_async_remote_copy(
                src_ref=zs.at[r, zz], dst_ref=zr.at[r, z], send_sem=zss.at[r], recv_sem=zsr.at[r],
                device_id=at(t, y * 8 + zz), device_id_type=MESH,
            ).start()
            return 0

        lax.fori_loop(1, 8, spread_z, 0)

    def owner(r, start):
        xx = rem(x + ROUND[r], 4)
        tt, pp = 2 * xx + rem(z, 2), 4 * t + y
        q = div(z, 2)
        dst = gwr.at[q]
        cp = remote(fin.at[r], dst, fs.at[r], fr.at[q], at(tt, pp), start=False)
        if r > 0:
            if start:
                cp.start()
            else:
                cp.wait_send()
            return
        me = jnp.logical_and(tt == t, pp == p)

        @pl.when(me)
        def _():
            if start:
                pltpu.make_async_copy(fin.at[r], dst, fr.at[q]).start()

        @pl.when(jnp.logical_not(me))
        def _():
            if start:
                cp.start()
            else:
                cp.wait_send()

    def z_sum(r):
        pltpu.make_async_copy(zr.at[r], zr.at[r], zsr.at[r]).wait()
        fin[r] = jnp.sum(zr[r].astype(F32), axis=0).astype(BF16)
        owner(r, True)

    def gm_add(xx, first):
        def rowblock(i, _):
            rows = pl.ds(pl.multiple_of(i * 256, 256), 256)
            v = lax.dot_general(gq[xx, rows, :], w[xx], (((1,), (1,)), ((), ())), preferred_element_type=F32)
            gmacc[rows, :] = v if first else gmacc[rows, :] + v
            return 0

        lax.fori_loop(0, 4, rowblock, 0)

    full = pl.ds(0, ROWS)
    cp_gq.wait()
    got(x, full, 1 - c, 4)
    partial(0)
    y_send(0)
    gathered_z(1)
    gather_z(2)
    y_pass(0)
    gathered_z(2)
    gather_z(3)
    got(x3, half(0), c, 0)
    remote(gq.at[x3, half(0), cols(c)], gq.at[x3, half(0), cols(c)], qs.at[5], qr.at[5], right)
    forward(x3, half(0), 7)
    got(x1, half(1), c, 1)
    remote(gq.at[x1, half(1), cols(c)], gq.at[x1, half(1), cols(c)], qs.at[6], qr.at[6], left)
    forward(x1, half(1), 8)
    got(x3, half(1), c, 2)
    forward(x3, half(1), 9)
    got(x1, half(0), c, 3)
    forward(x1, half(0), 10)
    z_send(0)
    got(x1, half(1), 1 - c, 8)
    got(x1, half(0), 1 - c, 10)
    partial(1)
    y_send(1)
    got(x3, half(0), 1 - c, 7)
    got(x3, half(1), 1 - c, 9)
    partial(2)
    y_send(2)
    gathered_z(3)
    for i in (1, 3, 2):
        arrived(wy(4 - i), ys.at[i], yr.at[i])
    gm_add(x, True)
    got(x2, half(0), c, 5)
    forward(x2, half(0), 11)
    got(x2, half(1), c, 6)
    forward(x2, half(1), 12)
    gm_add(x1, False)
    y_pass(1)
    got(x2, half(0), 1 - c, 11)
    got(x2, half(1), 1 - c, 12)
    partial(3)
    y_send(3)
    gm_add(x3, False)

    for k in (2, 1, 3, 0):
        xx = rem(x + k, 4)
        rows = pl.ds(pl.multiple_of(xx * 256, 256), 256)
        v = lax.dot_general(gq[x2, rows, :], w[x2], (((1,), (1,)), ((), ())), preferred_element_type=F32)
        v = gmacc[rows, :] + v
        gms[pl.ds(2 * xx, 2)] = v.astype(BF16).reshape(2, TOK, DS)
        for cc in range(2):
            tt = 2 * xx + (c if cc == 0 else 1 - c)
            if k == 0 and cc == 0:
                gmr[t] = gms[t]
            else:
                remote(gms.at[tt], gmr.at[t], gs.at[k, cc], gr.at[k, cc], at(tt, p))
    def spread_table(src, dst, k):
        pltpu.make_async_copy(src(z), dst.at[z], tre.at[k]).start()
        for i in range(1, 8):
            zz = rem(z + i, 8)
            pltpu.make_async_remote_copy(
                src_ref=src(zz), dst_ref=dst.at[z], send_sem=tse.at[k], recv_sem=tre.at[k],
                device_id=at(t, y * 8 + zz), device_id_type=MESH,
            ).start()

    y_pass(2)
    z_send(1)
    y_pass(3)
    gmv = gms[...].reshape(ROWS, DS)
    prod = (gmv.astype(F32) * nd[...].reshape(ROWS, DS).astype(F32)).astype(BF16)
    sums = jnp.dot(hot_shift, gmv, preferred_element_type=F32) + jnp.dot(hot_scale, prod, preferred_element_type=F32)
    tsum[...] = sums.reshape(8, 8, DS)
    spread_table(lambda zz: tsum.at[zz], tz, 0)
    z_send(2)
    z_send(3)
    z_sum(0)
    pltpu.make_async_copy(tz, tz, tre.at[0]).wait()
    tp[...] = jnp.sum(tz[...], axis=0)
    ty[y] = tp[...]
    for i in (1, 3, 2):
        remote(tp, ty.at[y], tys.at[i], tyr.at[i], at(t, zy(i, 0)))
    z_sum(1)
    z_sum(2)
    for i in (1, 3, 2):
        arrived(ty.at[rem(y + 4 - i, 4)], tys.at[i], tyr.at[i])
    tt_v[...] = ty[0] + ty[1] + ty[2] + ty[3]
    spread_table(lambda zz: tt_v, tfull, 1)
    z_sum(3)
    pltpu.make_async_copy(tfull, tfull, tre.at[1]).wait()
    tb[...] = tfull[...].reshape(2 * STEPS, DS).astype(BF16)

    def gt(tt):
        return gt_h.at[:, slice_cols(tt)]

    cp_gt = pltpu.make_async_copy(tb, gt(t), loc.at[6])
    cp_gt.start()
    for k in (2, 1, 3):
        remote(tb, gt(t), xs.at[k], xr_sem.at[k], at(xc(k, c), p))
    remote(tb, gt(t), xs.at[0], xr_sem.at[0], sib)

    for k in (1, 3, 2, 0):
        for cc in range(2):
            if k == 0 and cc == 0:
                continue
            arrived(gmr.at[2 * rem(x + 4 - k, 4) + (c if cc == 0 else 1 - c)], gs.at[k, cc], gr.at[k, cc])

    def back(i, _):
        rows = pl.ds(i * 16, 16)
        gn = [gmr[j, rows, :].astype(F32) * scl[rows, j * DS : (j + 1) * DS] for j in range(NT)]
        nv = [nrm32[rows, j * DS : (j + 1) * DS] for j in range(NT)]
        m1 = sum(jnp.sum(g, axis=-1, keepdims=True) for g in gn) * (1.0 / D)
        m2 = sum(jnp.sum(g * n, axis=-1, keepdims=True) for g, n in zip(gn, nv)) * (1.0 / D)
        k = inv[rows, 0:1]
        for j in range(NT):
            gxv[rows, j * DS : (j + 1) * DS] = ((gn[j] - m1 - nv[j] * m2) * k).astype(BF16)
        return 0

    lax.fori_loop(0, TOK // 16, back, 0)
    cp_gx = pltpu.make_async_copy(gxv, gx_h, loc.at[7])
    cp_gx.start()

    for k in (1, 3, 2):
        s = xc(4 - k, c)
        arrived(gt(s), xs.at[k], xr_sem.at[k])
        remote(gt(s), gt(s), xs.at[3 + k], xr_sem.at[3 + k], sib)

    for q in range(4):
        arrived(gwr.at[q], fs.at[0], fr.at[q])
    gwv[...] = gwr[...].astype(F32).reshape(PY, GW)
    cp_gw = pltpu.make_async_copy(gwv, gw_h, loc.at[8])
    cp_gw.start()
    arrived(gt(xc(0, 1 - c)), xs.at[0], xr_sem.at[0])
    for k in (1, 3, 2):
        s = xc(4 - k, 1 - c)
        arrived(gt(s), xs.at[3 + k], xr_sem.at[3 + k])
    cp_gt.wait()
    cp_gx.wait()
    cp_gw.wait()
    for cp in sent:
        cp.wait_send()
    for r in range(4):
        owner(r, False)
        pltpu.make_async_copy(zr.at[r, pl.ds(0, 7)], zr.at[r, pl.ds(0, 7)], zss.at[r]).wait()
    for k in range(2):
        pltpu.make_async_copy(tz.at[pl.ds(0, 7)], tz.at[pl.ds(0, 7)], tse.at[k]).wait()


def body(tokens, sample_id, timestep, step_table, weight, grad_q):
    any_spec = pl.BlockSpec(memory_space=pl.ANY)
    vmem_spec = pl.BlockSpec(memory_space=pltpu.VMEM)
    dma = pltpu.SemaphoreType.DMA
    grad_x, grad_weight, table = pl.pallas_call(
        kernel,
        name="fused_backward",
        out_shape=(
            jax.ShapeDtypeStruct((TOK, D), BF16),
            jax.ShapeDtypeStruct((PY, GW), F32),
            jax.ShapeDtypeStruct((2 * STEPS, D), BF16),
        ),
        in_specs=[any_spec, vmem_spec, vmem_spec, any_spec, any_spec, any_spec],
        out_specs=(any_spec, any_spec, any_spec),
        scratch_shapes=[
            pltpu.VMEM((TOK, D), BF16),
            pltpu.VMEM((TOK, D), F32),
            pltpu.VMEM((NT, TOK, DS), BF16),
            pltpu.VMEM((TOK, 128), F32),
            pltpu.VMEM((TOK, D), F32),
            pltpu.VMEM((STEPS, 2, D), F32),
            pltpu.VMEM((STEPS, 2, DS), F32),
            pltpu.VMEM((3 * STEPS, ROWS), BF16),
            pltpu.VMEM((NT, TOK, DS), BF16),
            pltpu.VMEM((DS, ROWS), BF16),
            pltpu.VMEM((4, ROWS, DS), BF16),
            pltpu.VMEM((4, DS, DS), BF16),
            pltpu.VMEM((4, DS, DS), BF16),
            pltpu.VMEM((2, 4, PY, GW), BF16),
            pltpu.VMEM((2, 4, PY, DS), BF16),
            pltpu.VMEM((4, 8, PZ, GW), BF16),
            pltpu.VMEM((4, 8, PZ, GW), BF16),
            pltpu.VMEM((4, PZ, GW), BF16),
            pltpu.VMEM((4, PZ, GW), BF16),
            pltpu.VMEM((PY, GW), F32),
            pltpu.VMEM((ROWS, DS), F32),
            pltpu.VMEM((NT, TOK, DS), BF16),
            pltpu.VMEM((NT, TOK, DS), BF16),
            pltpu.VMEM((TOK, D), BF16),
            pltpu.VMEM((8, 8, DS), F32),
            pltpu.VMEM((8, 8, DS), F32),
            pltpu.VMEM((8, DS), F32),
            pltpu.VMEM((4, 8, DS), F32),
            pltpu.VMEM((8, DS), F32),
            pltpu.VMEM((8, 8, DS), F32),
            pltpu.VMEM((2 * STEPS, DS), BF16),
            dma((9,)),
            dma((2, NT)), dma((2, NT)),
            dma((2, 4)), dma((2, 4)),
            dma((4,)), dma((4,)),
            dma((NT,)), dma((NT,)),
            dma((13,)), dma((13,)),
            dma((2, 4, 3)), dma((2, 4, 3)),
            dma((4,)), dma((4,)),
            dma((4,)), dma((4,)),
            dma((4, 2)), dma((4, 2)),
            dma((2,)), dma((2,)),
            dma((4,)), dma((4,)),
            dma((7,)), dma((7,)),
        ],
        cost_estimate=pl.CostEstimate(flops=9_700_000_000, bytes_accessed=14_000_000, transcendentals=0),
        compiler_params=pltpu.CompilerParams(
            collective_id=0, has_side_effects=True, vmem_limit_bytes=60 * 2**20
        ),
    )(tokens, sample_id, timestep, step_table, weight, grad_q)
    return (grad_x, grad_weight, table.astype(F32).reshape(STEPS, 2, D))


def solution(mesh):
    placed = (
        P(("dp", "tensor"), None),
        P("dp", None),
        P("dp", None),
        P(),
        P(None, "tensor"),
        P("dp", "tensor"),
    )
    return jax.shard_map(
        body,
        mesh=mesh,
        in_specs=placed,
        out_specs=(P(("dp", "tensor"), None), P("dp", "tensor"), P()),
        check_vma=False,
    )
```

```python
import jax
import jax.numpy as jnp
from jax import lax
from jax.experimental import pallas as pl
from jax.experimental.pallas import tpu as pltpu
from jax.sharding import PartitionSpec as P

MESH = pl.DeviceIdType.MESH
F32 = jnp.float32
BF16 = jnp.bfloat16

D = 6144
TOK = 128
ROWS = 1024
STEPS = 32
GW = 384
DS = 768
NT = 8
NDP = 32
WZ = 64
WY = 64
WYO = 512
PY = 192
PZ = 48
ROUND = (0, 1, 3, 2)


def rem(a, b):
    return lax.rem(a, jnp.int32(b))


def div(a, b):
    return lax.div(a, jnp.int32(b))


def kernel(
    tok_h, sid_ref, ts_ref, tab_h, w_h, gq_h,
    gx_h, gw_h, gt_h,
    tok, nrm32, nrm16, inv, scl, tab, tab_d, hot3, nd, modt, gq, w, part, y0, y1, zs, zr, fin, gwr, gwv,
    gmacc, gms, gmr, gxv, tsum, tz, tp, ty, tt_v, tfull, tb,
    loc, ws, wr, ags, agr, ys, yr, ns, nr, qs, qr, rss, rsr, zss, zsr, fs, fr, gs, gr, tse, tre, tys, tyr, xs, xr_sem,
):
    t = lax.axis_index("tensor")
    p = lax.axis_index("dp")
    x, c = div(t, 2), rem(t, 2)
    y, z = div(p, 8), rem(p, 8)

    def at(tt, pp):
        return {"tensor": tt, "dp": pp}

    def xc(dx, cc):
        return rem(x + dx, 4) * 2 + cc

    def zy(dy, dz):
        return rem(y + dy, 4) * 8 + rem(z + dz, 8)

    sent = []

    def remote(src, dst, s, r, dev, start=True):
        cp = pltpu.make_async_remote_copy(
            src_ref=src, dst_ref=dst, send_sem=s, recv_sem=r, device_id=dev, device_id_type=MESH
        )
        if start:
            cp.start()
            sent.append(cp)
        return cp

    def arrived(dst, s, r):
        pltpu.make_async_remote_copy(
            src_ref=dst, dst_ref=dst, send_sem=s, recv_sem=r, device_id=at(t, p), device_id_type=MESH
        ).wait_recv()

    bar = pltpu.get_barrier_semaphore()
    for i in range(1, NT):
        pl.semaphore_signal(bar, inc=1, device_id=at(rem(t + i, NT), p), device_id_type=MESH)

    for i in range(1, 8):
        pl.semaphore_signal(bar, inc=1, device_id=at(t, zy(0, i)), device_id_type=MESH)
    for i in range(1, 4):
        pl.semaphore_signal(bar, inc=1, device_id=at(t, zy(i, 0)), device_id_type=MESH)
    for q in range(4):
        pl.semaphore_signal(
            bar, inc=1, device_id=at(div(p, 4), rem(p, 4) * 8 + 2 * q + c), device_id_type=MESH
        )

    def cols(cc):
        return pl.ds(pl.multiple_of(cc * GW, GW), GW)

    def slice_cols(tt):
        return pl.ds(pl.multiple_of(tt * DS, DS), DS)

    cp_tok = pltpu.make_async_copy(tok_h, tok, loc.at[0])
    cp_tok.start()
    cp_tab = pltpu.make_async_copy(tab_h, tab, loc.at[1])
    cp_tab.start()
    cp_td = pltpu.make_async_copy(tab_h.at[:, :, slice_cols(t)], tab_d, loc.at[2])
    cp_td.start()
    cp_gq = pltpu.make_async_copy(gq_h, gq.at[x, :, cols(c)], loc.at[3])
    cp_gq.start()
    cp_wz = pltpu.make_async_copy(
        w_h.at[pl.ds(t * DS + z * WZ, WZ), :], w.at[x, pl.ds(z * WZ, WZ), cols(c)], loc.at[4]
    )
    cp_wz.start()
    cp_wy = pltpu.make_async_copy(
        w_h.at[pl.ds(t * DS + WYO + y * WY, WY), :], w.at[x, pl.ds(WYO + y * WY, WY), cols(c)], loc.at[5]
    )
    cp_wy.start()

    pl.semaphore_wait(bar, NT - 1 + 7 + 3 + 4)

    for i in range(1, NT):
        tt = rem(t + i, NT)
        remote(
            w_h.at[pl.ds(tt * DS + z * WZ, WZ), :], w.at[x, pl.ds(z * WZ, WZ), cols(c)],
            ws.at[0, i], wr.at[0, i], at(tt, p),
        )
        remote(
            w_h.at[pl.ds(tt * DS + WYO + y * WY, WY), :], w.at[x, pl.ds(WYO + y * WY, WY), cols(c)],
            ws.at[1, i], wr.at[1, i], at(tt, p),
        )

    cp_tok.wait()

    def norm(i, _):
        rows = pl.ds(i * 16, 16)
        v = tok[rows, :].astype(F32)
        v = v - jnp.mean(v, axis=-1, keepdims=True)
        k = lax.rsqrt(jnp.mean(v * v, axis=-1, keepdims=True) + 1e-06)
        v = v * k
        nrm32[rows, :] = v
        inv[rows, :] = jnp.broadcast_to(k, (16, 128))
        for j in range(NT):
            nrm16[j, rows, :] = v[:, j * DS : (j + 1) * DS].astype(BF16)
        return 0

    lax.fori_loop(0, TOK // 16, norm, 0)
    for i in (4, 5, 2, 3, 6, 7, 1):
        tt = rem(t + i, NT)
        remote(nrm16.at[tt], nd.at[t], ns.at[i], nr.at[i], at(tt, p))
    nd[t] = nrm16[t]

    def half(h):
        return pl.ds(h * 512, 512)

    right, left, sib = at(xc(1, c), p), at(xc(3, c), p), at(xc(0, 1 - c), p)

    step = jnp.zeros((1, ROWS), jnp.int32)
    for s in range(8):
        step = step + jnp.where(sid_ref[...] == s, ts_ref[0:1, s : s + 1], 0)
    level = lax.broadcasted_iota(jnp.int32, (2 * STEPS, ROWS), 0)
    hot_shift = (level == 2 * step).astype(F32).astype(BF16)
    hot_scale = (level == 2 * step + 1).astype(F32).astype(BF16)
    hot = (lax.broadcasted_iota(jnp.int32, (STEPS, ROWS), 0) == step).astype(F32).astype(BF16)
    for k in range(3):
        hot3[k * STEPS : (k + 1) * STEPS, :] = hot

    def thirds(v):
        hi = v.astype(BF16)
        rest = v - hi.astype(F32)
        mid = rest.astype(BF16)
        lo = (rest - mid.astype(F32)).astype(BF16)
        return jnp.concatenate([hi, mid, lo], axis=0)

    def pick(h, table):
        return lax.dot_general(h, thirds(table), (((0,), (0,)), ((), ())), preferred_element_type=F32)

    cp_tab.wait()
    own = hot3[:, pl.ds(pl.multiple_of(t * TOK, TOK), TOK)]
    for j in range(NT):
        js = slice(j * DS, (j + 1) * DS)
        scl[:, js] = pick(own, 1.0 + tab[:, 1, js])

    def forward(xx, hh, k):
        v = gq.at[xx, hh, cols(c)]
        remote(v, v, qs.at[k], qr.at[k], sib)

    def got(xx, hh, cc, k):
        arrived(gq.at[xx, hh, cols(cc)], qs.at[k], qr.at[k])

    x1, x2, x3 = rem(x + 1, 4), rem(x + 2, 4), rem(x + 3, 4)

    def arrived_rows(which):
        for i in which:
            arrived(nd.at[rem(t + NT - i, NT)], ns.at[i], nr.at[i])

    cp_wz.wait()
    for i in range(1, NT):
        s = rem(t + NT - i, NT)
        arrived(w.at[div(s, 2), pl.ds(z * WZ, WZ), cols(rem(s, 2))], ws.at[0, i], wr.at[0, i])

    def wz(d, k=None):
        r = pl.ds(rem(z + d + 8, 8) * WZ, WZ)
        return w.at[:, r, :] if k is None else w.at[pl.ds(2 * k, 2), r, :]

    def gather_z(s):
        a, b = (wz(-s), wz(s)) if s < 3 else (wz(-s, 0), wz(s, 1))
        remote(a, a, ags.at[0, s], agr.at[0, s], at(t, zy(0, 1)))
        remote(b, b, ags.at[1, s], agr.at[1, s], at(t, zy(0, 7)))

    def gathered_z(s):
        a, b = (wz(-1 - s), wz(1 + s)) if s < 3 else (wz(-1 - s, 0), wz(1 + s, 1))
        arrived(a, ags.at[0, s], agr.at[0, s])
        arrived(b, ags.at[1, s], agr.at[1, s])

    def wy(d):
        return w.at[:, pl.ds(WYO + rem(y + d, 4) * WY, WY), :]

    gather_z(0)
    cp_wy.wait()
    for i in range(1, NT):
        s = rem(t + NT - i, NT)
        arrived(w.at[div(s, 2), pl.ds(WYO + y * WY, WY), cols(rem(s, 2))], ws.at[1, i], wr.at[1, i])
    for i in (1, 3, 2):
        remote(wy(0), wy(0), ys.at[i], yr.at[i], at(t, zy(i, 0)))
    arrived_rows((2, 6))
    remote(gq_h.at[half(0), :], gq.at[x, half(0), cols(c)], qs.at[0], qr.at[0], right)
    remote(gq_h.at[half(1), :], gq.at[x, half(1), cols(c)], qs.at[1], qr.at[1], left)
    remote(gq_h.at[half(1), :], gq.at[x, half(1), cols(c)], qs.at[2], qr.at[2], right)
    remote(gq_h.at[half(0), :], gq.at[x, half(0), cols(c)], qs.at[3], qr.at[3], left)
    remote(gq_h, gq.at[x, :, cols(c)], qs.at[4], qr.at[4], sib)
    gathered_z(0)
    gather_z(1)

    arrived_rows((1, 3, 4, 5, 7))
    cp_td.wait()
    shift3 = thirds(tab_d[:, 0, :])
    scale3 = thirds(1.0 + tab_d[:, 1, :])

    for i in range(4):
        h = hot3[:, i * 256 : (i + 1) * 256]
        sh = lax.dot_general(h, shift3, (((0,), (0,)), ((), ())), preferred_element_type=F32)
        sc = lax.dot_general(h, scale3, (((0,), (0,)), ((), ())), preferred_element_type=F32)
        m = nd[2 * i : 2 * i + 2].reshape(256, DS).astype(F32) * sc + sh
        modt[:, i * 256 : (i + 1) * 256] = m.T.astype(BF16)

    def partial(r):
        xx = rem(x + ROUND[r], 4)

        def rowblock(i, _):
            rows = pl.ds(pl.multiple_of(i * 256, 256), 256)
            part[r, rows, :] = jnp.dot(modt[rows, :], gq[xx], preferred_element_type=F32).astype(BF16)
            return 0

        lax.fori_loop(0, 3, rowblock, 0)

    A, B = slice(0, GW), slice(GW, DS)
    up, down = at(t, zy(1, 0)), at(t, zy(3, 0))

    def piece(d):
        return pl.ds(pl.multiple_of(rem(y + d, 4) * PY, PY), PY)

    def y_send(r):
        for k, (d, cc, dst, dev) in enumerate(
            ((2, A, y0.at[0, r], up), (1, B, y1.at[0, r, :, B], up))
        ):
            remote(part.at[r, piece(d), cc], dst, rss.at[0, r, k], rsr.at[0, r, k], dev)
        for k, (d, cc, dst, dev) in enumerate(
            ((2, B, y0.at[1, r], down), (3, A, y1.at[1, r, :, A], down))
        ):
            remote(part.at[r, piece(d), cc], dst, rss.at[1, r, k], rsr.at[1, r, k], dev)

    def y_pass(r):
        for k, (d, cc, dev) in enumerate(((1, A, up), (3, B, down))):
            arrived(y0.at[k, r], rss.at[k, r, 0], rsr.at[k, r, 0])
            v = part[r, piece(d), cc].astype(F32) + y0[k, r].astype(F32)
            part[r, piece(d), cc] = v.astype(BF16)
            remote(part.at[r, piece(d), cc], y1.at[k, r, :, cc], rss.at[k, r, 2], rsr.at[k, r, 2], dev)

    def z_send(r):
        for k, (early, late) in enumerate(((B, A), (A, B))):
            arrived(y1.at[k, r, :, early], rss.at[k, r, 1], rsr.at[k, r, 1])
            arrived(y1.at[k, r, :, late], rss.at[k, r, 2], rsr.at[k, r, 2])
        v = part[r, piece(0), :].astype(F32) + y1[0, r].astype(F32) + y1[1, r].astype(F32)
        for k in range(8):
            rows, cc = slice((k // 2) * PZ, (k // 2 + 1) * PZ), (A, B)[k % 2]
            zs[r, k] = v[rows, cc].astype(BF16)
        pltpu.make_async_copy(zs.at[r, z], zr.at[r, z], zsr.at[r]).start()

        def spread_z(i, _):
            zz = rem(z + i, 8)
            pltpu.make_async_remote_copy(
                src_ref=zs.at[r, zz], dst_ref=zr.at[r, z], send_sem=zss.at[r], recv_sem=zsr.at[r],
                device_id=at(t, y * 8 + zz), device_id_type=MESH,
            ).start()
            return 0

        lax.fori_loop(1, 8, spread_z, 0)

    def owner(r, start):
        xx = rem(x + ROUND[r], 4)
        tt, pp = 2 * xx + rem(z, 2), 4 * t + y
        q = div(z, 2)
        dst = gwr.at[q]
        cp = remote(fin.at[r], dst, fs.at[r], fr.at[q], at(tt, pp), start=False)
        if r > 0:
            if start:
                cp.start()
            else:
                cp.wait_send()
            return
        me = jnp.logical_and(tt == t, pp == p)

        @pl.when(me)
        def _():
            if start:
                pltpu.make_async_copy(fin.at[r], dst, fr.at[q]).start()

        @pl.when(jnp.logical_not(me))
        def _():
            if start:
                cp.start()
            else:
                cp.wait_send()

    def z_sum(r):
        pltpu.make_async_copy(zr.at[r], zr.at[r], zsr.at[r]).wait()
        fin[r] = jnp.sum(zr[r].astype(F32), axis=0).astype(BF16)
        owner(r, True)

    def gm_add(xx, first):
        def rowblock(i, _):
            rows = pl.ds(pl.multiple_of(i * 256, 256), 256)
            v = lax.dot_general(gq[xx, rows, :], w[xx], (((1,), (1,)), ((), ())), preferred_element_type=F32)
            gmacc[rows, :] = v if first else gmacc[rows, :] + v
            return 0

        lax.fori_loop(0, 4, rowblock, 0)

    full = pl.ds(0, ROWS)
    cp_gq.wait()
    got(x, full, 1 - c, 4)
    partial(0)
    y_send(0)
    gathered_z(1)
    gather_z(2)
    y_pass(0)
    gathered_z(2)
    gather_z(3)
    got(x3, half(0), c, 0)
    remote(gq.at[x3, half(0), cols(c)], gq.at[x3, half(0), cols(c)], qs.at[5], qr.at[5], right)
    forward(x3, half(0), 7)
    got(x1, half(1), c, 1)
    remote(gq.at[x1, half(1), cols(c)], gq.at[x1, half(1), cols(c)], qs.at[6], qr.at[6], left)
    forward(x1, half(1), 8)
    got(x3, half(1), c, 2)
    forward(x3, half(1), 9)
    got(x1, half(0), c, 3)
    forward(x1, half(0), 10)
    z_send(0)
    got(x1, half(1), 1 - c, 8)
    got(x1, half(0), 1 - c, 10)
    partial(1)
    y_send(1)
    got(x3, half(0), 1 - c, 7)
    got(x3, half(1), 1 - c, 9)
    partial(2)
    y_send(2)
    gathered_z(3)
    for i in (1, 3, 2):
        arrived(wy(4 - i), ys.at[i], yr.at[i])
    gm_add(x, True)
    got(x2, half(0), c, 5)
    forward(x2, half(0), 11)
    got(x2, half(1), c, 6)
    forward(x2, half(1), 12)
    gm_add(x1, False)
    y_pass(1)
    got(x2, half(0), 1 - c, 11)
    got(x2, half(1), 1 - c, 12)
    gm_add(x3, False)

    for k in (2, 1, 3, 0):
        xx = rem(x + k, 4)
        rows = pl.ds(pl.multiple_of(xx * 256, 256), 256)
        v = lax.dot_general(gq[x2, rows, :], w[x2], (((1,), (1,)), ((), ())), preferred_element_type=F32)
        v = gmacc[rows, :] + v
        gms[pl.ds(2 * xx, 2)] = v.astype(BF16).reshape(2, TOK, DS)
        for cc in range(2):
            tt = 2 * xx + (c if cc == 0 else 1 - c)
            if k == 0 and cc == 0:
                gmr[t] = gms[t]
            else:
                remote(gms.at[tt], gmr.at[t], gs.at[k, cc], gr.at[k, cc], at(tt, p))
    def spread_table(src, dst, k):
        pltpu.make_async_copy(src(z), dst.at[z], tre.at[k]).start()
        for i in range(1, 8):
            zz = rem(z + i, 8)
            pltpu.make_async_remote_copy(
                src_ref=src(zz), dst_ref=dst.at[z], send_sem=tse.at[k], recv_sem=tre.at[k],
                device_id=at(t, y * 8 + zz), device_id_type=MESH,
            ).start()

    gmv = gms[...].reshape(ROWS, DS)
    prod = (gmv.astype(F32) * nd[...].reshape(ROWS, DS).astype(F32)).astype(BF16)
    sums = jnp.dot(hot_shift, gmv, preferred_element_type=F32) + jnp.dot(hot_scale, prod, preferred_element_type=F32)
    tsum[...] = sums.reshape(8, 8, DS)
    spread_table(lambda zz: tsum.at[zz], tz, 0)
    partial(3)
    y_send(3)
    y_pass(2)
    z_send(1)
    pltpu.make_async_copy(tz, tz, tre.at[0]).wait()
    tp[...] = jnp.sum(tz[...], axis=0)
    ty[y] = tp[...]
    for i in (1, 3, 2):
        remote(tp, ty.at[y], tys.at[i], tyr.at[i], at(t, zy(i, 0)))
    y_pass(3)
    z_send(2)
    for i in (1, 3, 2):
        arrived(ty.at[rem(y + 4 - i, 4)], tys.at[i], tyr.at[i])
    tt_v[...] = ty[0] + ty[1] + ty[2] + ty[3]
    spread_table(lambda zz: tt_v, tfull, 1)
    z_sum(0)
    z_send(3)
    z_sum(1)
    pltpu.make_async_copy(tfull, tfull, tre.at[1]).wait()
    tb[...] = tfull[...].reshape(2 * STEPS, DS).astype(BF16)

    def gt(tt):
        return gt_h.at[:, slice_cols(tt)]

    cp_gt = pltpu.make_async_copy(tb, gt(t), loc.at[6])
    cp_gt.start()
    for k in (2, 1, 3):
        remote(tb, gt(t), xs.at[k], xr_sem.at[k], at(xc(k, c), p))
    remote(tb, gt(t), xs.at[0], xr_sem.at[0], sib)
    z_sum(2)
    z_sum(3)
    for k in (1, 3, 2):
        u = xc(4 - k, c)
        arrived(gt(u), xs.at[k], xr_sem.at[k])
        remote(gt(u), gt(u), xs.at[3 + k], xr_sem.at[3 + k], sib)

    for k in (1, 3, 2, 0):
        for cc in range(2):
            if k == 0 and cc == 0:
                continue
            arrived(gmr.at[2 * rem(x + 4 - k, 4) + (c if cc == 0 else 1 - c)], gs.at[k, cc], gr.at[k, cc])

    def back(i, _):
        rows = pl.ds(i * 16, 16)
        gn = [gmr[j, rows, :].astype(F32) * scl[rows, j * DS : (j + 1) * DS] for j in range(NT)]
        nv = [nrm32[rows, j * DS : (j + 1) * DS] for j in range(NT)]
        m1 = sum(jnp.sum(g, axis=-1, keepdims=True) for g in gn) * (1.0 / D)
        m2 = sum(jnp.sum(g * n, axis=-1, keepdims=True) for g, n in zip(gn, nv)) * (1.0 / D)
        k = inv[rows, 0:1]
        for j in range(NT):
            gxv[rows, j * DS : (j + 1) * DS] = ((gn[j] - m1 - nv[j] * m2) * k).astype(BF16)
        return 0

    lax.fori_loop(0, TOK // 16, back, 0)
    cp_gx = pltpu.make_async_copy(gxv, gx_h, loc.at[7])
    cp_gx.start()

    for q in range(4):
        arrived(gwr.at[q], fs.at[0], fr.at[q])
    gwv[...] = gwr[...].astype(F32).reshape(PY, GW)
    cp_gw = pltpu.make_async_copy(gwv, gw_h, loc.at[8])
    cp_gw.start()
    arrived(gt(xc(0, 1 - c)), xs.at[0], xr_sem.at[0])
    for k in (1, 3, 2):
        s = xc(4 - k, 1 - c)
        arrived(gt(s), xs.at[3 + k], xr_sem.at[3 + k])
    cp_gt.wait()
    cp_gx.wait()
    cp_gw.wait()
    for cp in sent:
        cp.wait_send()
    for r in range(4):
        owner(r, False)
        pltpu.make_async_copy(zr.at[r, pl.ds(0, 7)], zr.at[r, pl.ds(0, 7)], zss.at[r]).wait()
    for k in range(2):
        pltpu.make_async_copy(tz.at[pl.ds(0, 7)], tz.at[pl.ds(0, 7)], tse.at[k]).wait()


def body(tokens, sample_id, timestep, step_table, weight, grad_q):
    any_spec = pl.BlockSpec(memory_space=pl.ANY)
    vmem_spec = pl.BlockSpec(memory_space=pltpu.VMEM)
    dma = pltpu.SemaphoreType.DMA
    grad_x, grad_weight, table = pl.pallas_call(
        kernel,
        name="fused_backward",
        out_shape=(
            jax.ShapeDtypeStruct((TOK, D), BF16),
            jax.ShapeDtypeStruct((PY, GW), F32),
            jax.ShapeDtypeStruct((2 * STEPS, D), BF16),
        ),
        in_specs=[any_spec, vmem_spec, vmem_spec, any_spec, any_spec, any_spec],
        out_specs=(any_spec, any_spec, any_spec),
        scratch_shapes=[
            pltpu.VMEM((TOK, D), BF16),
            pltpu.VMEM((TOK, D), F32),
            pltpu.VMEM((NT, TOK, DS), BF16),
            pltpu.VMEM((TOK, 128), F32),
            pltpu.VMEM((TOK, D), F32),
            pltpu.VMEM((STEPS, 2, D), F32),
            pltpu.VMEM((STEPS, 2, DS), F32),
            pltpu.VMEM((3 * STEPS, ROWS), BF16),
            pltpu.VMEM((NT, TOK, DS), BF16),
            pltpu.VMEM((DS, ROWS), BF16),
            pltpu.VMEM((4, ROWS, DS), BF16),
            pltpu.VMEM((4, DS, DS), BF16),
            pltpu.VMEM((4, DS, DS), BF16),
            pltpu.VMEM((2, 4, PY, GW), BF16),
            pltpu.VMEM((2, 4, PY, DS), BF16),
            pltpu.VMEM((4, 8, PZ, GW), BF16),
            pltpu.VMEM((4, 8, PZ, GW), BF16),
            pltpu.VMEM((4, PZ, GW), BF16),
            pltpu.VMEM((4, PZ, GW), BF16),
            pltpu.VMEM((PY, GW), F32),
            pltpu.VMEM((ROWS, DS), F32),
            pltpu.VMEM((NT, TOK, DS), BF16),
            pltpu.VMEM((NT, TOK, DS), BF16),
            pltpu.VMEM((TOK, D), BF16),
            pltpu.VMEM((8, 8, DS), F32),
            pltpu.VMEM((8, 8, DS), F32),
            pltpu.VMEM((8, DS), F32),
            pltpu.VMEM((4, 8, DS), F32),
            pltpu.VMEM((8, DS), F32),
            pltpu.VMEM((8, 8, DS), F32),
            pltpu.VMEM((2 * STEPS, DS), BF16),
            dma((9,)),
            dma((2, NT)), dma((2, NT)),
            dma((2, 4)), dma((2, 4)),
            dma((4,)), dma((4,)),
            dma((NT,)), dma((NT,)),
            dma((13,)), dma((13,)),
            dma((2, 4, 3)), dma((2, 4, 3)),
            dma((4,)), dma((4,)),
            dma((4,)), dma((4,)),
            dma((4, 2)), dma((4, 2)),
            dma((2,)), dma((2,)),
            dma((4,)), dma((4,)),
            dma((7,)), dma((7,)),
        ],
        cost_estimate=pl.CostEstimate(flops=9_700_000_000, bytes_accessed=14_000_000, transcendentals=0),
        compiler_params=pltpu.CompilerParams(
            collective_id=0, has_side_effects=True, vmem_limit_bytes=60 * 2**20
        ),
    )(tokens, sample_id, timestep, step_table, weight, grad_q)
    return (grad_x, grad_weight, table.astype(F32).reshape(STEPS, 2, D))


def solution(mesh):
    placed = (
        P(("dp", "tensor"), None),
        P("dp", None),
        P("dp", None),
        P(),
        P(None, "tensor"),
        P("dp", "tensor"),
    )
    return jax.shard_map(
        body,
        mesh=mesh,
        in_specs=placed,
        out_specs=(P(("dp", "tensor"), None), P("dp", "tensor"), P()),
        check_vma=False,
    )
```
